512 devices in a mesh: aux: 64 (over x, z), ao: 8 (over y, core).
Axes of the slice: x: 4, y: 4, z: 16, core: 2. Of those that a mesh axis runs over, the one named last changes fastest.
Arguments:
- pair_integrals: bfloat16 [64, 192, 128, 128], P('aux', 'ao'), may hold values from -6 to 6
- occ_coef: bfloat16 [320, 6144], replicated, may hold values from -0.5 to 0.5
- vir_coef: bfloat16 [6144, 5760], P('aux', 'ao'), may hold values from -0.078125 to 0.078125
- metric_factor: bfloat16 [64, 64], replicated, may hold values from -0.75 to 0.75
- block_rows: int32 [192], replicated, may hold values from 0 to 47, as said below
- block_cols: int32 [192], replicated, may hold values from 0 to 47, as said below
- block_count: int32 [8], replicated, may hold values from 6 to 24, as said below
- occ_order: int32 [320], replicated, may hold values from 0 to 319, each once
Outputs:
- factor_b: bfloat16 [64, 320, 5760], P(None, 'aux', 'ao')
The draws below stay inside these ranges and needn't reach their ends.
Inputs may be any that keep to these rules, and one draw needn't show every extreme that they name: `block_rows`: slots of row group g name row blocks g * 6 to (g + 1) * 6 - 1; within a group no (row, column) pair repeats. `block_cols`: column blocks of any row group, in any order. `block_count`: exactly one row group fills all 24 slots in every draw.
All inputs are finite; a program needn't handle non-finite values.
Results may differ from the reference program's by a relative error of at most 0.017.
Values may be sent and summed in bfloat16 or wider, within the bound.
No kernel may reach another device: no remote copies, remote signals or barrier semaphores. Data moves between devices by JAX's collectives and lax.ppermute only.
A program may use at most 128 MiB of HBM per device.

```python
import jax
import jax.numpy as jnp
from jax import lax

AO = 6144
BS = 128
OCC = 320
VIR = 5760
NAUX = 64
NBLK = 48
RB = 6
SLOTS = 24
N_AO = 8


def screened_pattern(key):
    pairs = RB * NBLK
    group_keys = jax.random.split(jax.random.fold_in(key, 101), N_AO)

    def pick_group(one):
        rest = jax.random.permutation(one, pairs - 2)[:SLOTS - 2] + 1
        fixed = jnp.array([pairs - 1, 0], dtype=jnp.int32)
        return jnp.concatenate([fixed, rest.astype(jnp.int32)])
    picks = jax.vmap(pick_group)(group_keys)
    groups = jnp.arange(N_AO, dtype=jnp.int32)[:, None]
    rows = (groups * RB + picks // NBLK).reshape(-1).astype(jnp.int32)
    cols = (picks % NBLK).reshape(-1).astype(jnp.int32)
    heavy = jax.random.randint(jax.random.fold_in(key, 102), (), 0, N_AO)
    light = jax.random.randint(jax.random.fold_in(key, 103), (N_AO,), SLOTS // 4, SLOTS // 2 + 1)
    counts = jnp.where(jnp.arange(N_AO) == heavy, SLOTS, light).astype(jnp.int32)
    return (rows, cols, counts)


def draw_block_rows(key, part):
    pattern = screened_pattern(key)
    return pattern[0]


def draw_block_cols(key, part):
    pattern = screened_pattern(key)
    return pattern[1]


def draw_block_count(key, part):
    pattern = screened_pattern(key)
    return pattern[2]


def block_levels(rng, shape, cuts, low, high):
    factor_of, own = 1.0, jax.random.fold_in(rng, 6)
    for dim, shards_of in cuts:
        steps = jnp.exp(jax.random.uniform(jax.random.fold_in(own, dim), (shards_of,), jnp.float32, low / len(cuts), high / len(cuts)))
        factor_of = factor_of * jnp.repeat(steps, shape[dim] // shards_of).reshape([-1 if axis == dim else 1 for axis in range(len(shape))])
    return factor_of


def noise(stream_key, shape, deviation, most, shards=(), kind=jnp.bfloat16):
    loudness = block_levels(stream_key, shape, shards, -0.22, 0.18) if shards else 1.0
    entries = jax.random.normal(stream_key, shape, jnp.float32) * deviation * loudness
    return jnp.minimum(jnp.maximum(entries, -most), most).astype(kind)


def setup_inputs(seed: int = 0) -> dict:
    arg_keys = jax.random.split(jax.random.key(seed), 9)
    pair_integrals = noise(arg_keys[0], (NAUX, N_AO * SLOTS, BS, BS), 1.0, 6.0, ((0, 64), (1, 8)))
    occ_coef = noise(arg_keys[1], (OCC, AO), BS ** -0.5, 0.5)
    vir_coef = noise(arg_keys[2], (AO, VIR), AO ** -0.5, 0.078125, ((0, 64), (1, 8)))
    metric_factor = noise(arg_keys[3], (NAUX, NAUX), NAUX ** -0.5, 0.75)
    block_rows = draw_block_rows(jax.random.fold_in(arg_keys[8], 71), 0)
    block_cols = draw_block_cols(jax.random.fold_in(arg_keys[8], 71), 0)
    block_count = draw_block_count(jax.random.fold_in(arg_keys[8], 71), 0)
    occ_order = jax.random.permutation(arg_keys[7], OCC).astype(jnp.int32)
    return dict(pair_integrals=pair_integrals, occ_coef=occ_coef, vir_coef=vir_coef, metric_factor=metric_factor, block_rows=block_rows, block_cols=block_cols, block_count=block_count, occ_order=occ_order)


def group_partial(blocks, occ_coef, block_rows, block_cols, count, base):
    width = blocks.shape[-1]

    def step(slot, total):
        index = (base + slot).astype(jnp.int32)
        row = block_rows[index].astype(jnp.int32)
        col = block_cols[index].astype(jnp.int32)
        coef = lax.dynamic_slice_in_dim(occ_coef, row * width, width, 1).astype(jnp.float32)
        block = lax.dynamic_index_in_dim(blocks, slot.astype(jnp.int32), 1, keepdims=False).astype(jnp.float32)
        term = jnp.einsum("im,pmn->pin", coef, block, precision=lax.Precision.HIGHEST)
        old = lax.dynamic_slice_in_dim(total, col * width, width, 2)
        return lax.dynamic_update_slice_in_dim(total, old + term, col * width, 2)

    start = jnp.zeros((blocks.shape[0], occ_coef.shape[0], occ_coef.shape[1]), jnp.float32)
    return lax.fori_loop(jnp.int32(0), count.astype(jnp.int32), step, start)


def reference(pair_integrals, occ_coef, vir_coef, metric_factor, block_rows, block_cols, block_count, occ_order):
    summed = jnp.zeros((NAUX, OCC, AO), jnp.float32)
    for group in range(N_AO):
        blocks = pair_integrals[:, group * SLOTS:(group + 1) * SLOTS]
        part = group_partial(blocks, occ_coef, block_rows, block_cols, block_count[group], jnp.int32(group * SLOTS))
        rounded = lax.optimization_barrier(part.astype(jnp.bfloat16))
        summed = summed + rounded.astype(jnp.float32)
    half = summed.astype(jnp.bfloat16)
    pencil = jnp.dot(half.reshape(NAUX * OCC, AO), vir_coef, preferred_element_type=jnp.float32)
    pencil = pencil.astype(jnp.bfloat16).reshape(NAUX, OCC, VIR)
    chosen = jnp.take(pencil, occ_order.astype(jnp.int32), axis=1)
    mixed = jnp.dot(metric_factor, chosen.reshape(NAUX, OCC * VIR), preferred_element_type=jnp.float32)
    return mixed.astype(jnp.bfloat16).reshape(NAUX, OCC, VIR)
```

```python
import jax
import jax.numpy as jnp
from jax import lax
from jax.experimental import pallas as pl
from jax.experimental.pallas import tpu as pltpu
from jax.sharding import Mesh, PartitionSpec as P

GROUP_ROWS = 6


def partial_kernel(
    rows, cols, counts, place, own, other, occ, order, out, total, coef, *, slots, width, blocks_x
):
    y, core = place[0], place[1]
    occ_width = occ.shape[0]
    half_blocks = blocks_x // 2
    pick = lax.broadcasted_iota(jnp.int32, (occ_width, occ_width), 1) == order[...]
    pick = jnp.where(pick, 1.0, 0.0).astype(jnp.bfloat16)
    for row in range(coef.shape[0]):
        chosen = jnp.dot(
            pick, occ[:, row * width : (row + 1) * width], preferred_element_type=jnp.float32
        )
        coef[row] = chosen.astype(jnp.bfloat16)
    total[...] = jnp.zeros_like(total)

    for which, blocks in ((core, own), (1 - core, other)):
        group = 2 * y + which

        @pl.loop(0, counts[group])
        def _(slot):
            col = cols[group * slots + slot]
            inside = lax.rem(col, blocks_x)

            @pl.when(inside // half_blocks == core)
            def _():
                row = rows[group * slots + slot] - 2 * y * GROUP_ROWS
                local = (col // blocks_x) * half_blocks + lax.rem(inside, half_blocks)
                total[local] += jnp.dot(
                    coef[row], blocks[slot], preferred_element_type=jnp.float32
                )

    for block in range(total.shape[0]):
        out[:, block * width : (block + 1) * width] = total[block].astype(out.dtype)


def group_partial(own, other, occ_coef, order, rows, cols, counts, place, blocks_x):
    slots, width = own.shape[0], own.shape[1]
    occ_width, ao_width = occ_coef.shape
    half_blocks = ao_width // width // 2
    kernel = lambda *refs: partial_kernel(*refs, slots=slots, width=width, blocks_x=blocks_x)
    whole = lambda *shape: pl.BlockSpec(shape, lambda i, *_: (0,) * len(shape))
    return pl.pallas_call(
        kernel,
        grid_spec=pltpu.PrefetchScalarGridSpec(
            num_scalar_prefetch=4,
            grid=(1,),
            in_specs=[
                whole(slots, width, width),
                whole(slots, width, width),
                pl.BlockSpec(
                    (occ_width, 2 * GROUP_ROWS * width), lambda i, r, c, n, place: (0, place[0])
                ),
                whole(occ_width, 1),
            ],
            out_specs=whole(occ_width, half_blocks * width),
            scratch_shapes=[
                pltpu.VMEM((half_blocks, occ_width, width), jnp.float32),
                pltpu.VMEM((2 * GROUP_ROWS, occ_width, width), jnp.bfloat16),
            ],
        ),
        out_shape=jax.ShapeDtypeStruct((occ_width, half_blocks * width), jnp.bfloat16),
        compiler_params=pltpu.CompilerParams(vmem_limit_bytes=40 << 20),
        name="group_partial",
    )(rows, cols, counts, place, own, other, occ_coef, order)


def shift(value, axis, step):
    n = lax.axis_size(axis)
    return lax.ppermute(value, axis, [(i, (i + step) % n) for i in range(n)])


def add(*terms):
    total = terms[0].astype(jnp.float32)
    for term in terms[1:]:
        total = total + term.astype(jnp.float32)
    return total.astype(jnp.bfloat16)


def scatter_sum(chunk, axis):
    far = chunk(2)
    cut = far.shape[0] // 2
    from_left = shift(far[:cut], axis, 1)
    from_right = shift(far[cut:], axis, -1)
    right, left = chunk(1), chunk(3)
    right = jnp.concatenate([add(right[:cut], from_left), right[cut:]], 0)
    left = jnp.concatenate([left[:cut], add(left[cut:], from_right)], 0)
    return add(chunk(0), shift(right, axis, 1), shift(left, axis, -1))


def gather_ring(mine, axis):
    left = shift(mine, axis, 1)
    right = shift(mine, axis, -1)
    cut = mine.shape[0] // 2
    far = jnp.concatenate([shift(left[:cut], axis, 1), shift(right[cut:], axis, -1)], 0)
    return mine, right, far, left


def shards(
    pair_integrals,
    occ_coef,
    vir_coef,
    metric_factor,
    block_rows,
    block_cols,
    block_count,
    occ_order,
):
    x, y, core = lax.axis_index("x"), lax.axis_index("y"), lax.axis_index("c")
    nx, nz, ny = lax.axis_size("x"), lax.axis_size("z"), lax.axis_size("y")
    width = pair_integrals.shape[2]
    occ_width, ao_width = occ_coef.shape
    vir_width = vir_coef.shape[1]
    naux = nx * nz
    each = occ_width // naux
    blocks_x = ao_width // width // nx
    half_blocks = blocks_x // 2

    vir_rows = lax.all_gather(vir_coef, "z", axis=0, tiled=True)
    deep = vir_rows.shape[0] // 2
    vir_rows = jnp.concatenate(
        [
            lax.dynamic_slice_in_dim(vir_rows, core * deep, deep, 0),
            lax.dynamic_slice_in_dim(vir_rows, (1 - core) * deep, deep, 0),
        ],
        0,
    )

    own = pair_integrals[0]
    other = shift(own, "c", 1)
    order = occ_order.reshape(nx, nz, each).transpose(0, 2, 1).reshape(occ_width, 1)
    place = jnp.stack([y, core]).astype(jnp.int32)
    part = group_partial(
        own, other, occ_coef, order, block_rows, block_cols, block_count, place, blocks_x
    )
    part = part.reshape(ny, occ_width // ny, part.shape[1])
    share = scatter_sum(
        lambda d: lax.dynamic_index_in_dim(part, lax.rem(y + d, ny), 0, keepdims=False), "y"
    )
    send = share.reshape(each, nz, nx, half_blocks, width).transpose(2, 1, 0, 3, 4)
    send = send.reshape(naux, each * half_blocks, width)
    got = lax.all_to_all(send, ("x", "z"), 0, 0, tiled=True)
    mine = got.reshape(naux, each, half_blocks, width).transpose(1, 0, 2, 3)
    mine = mine.reshape(each * naux, half_blocks * width)
    pieces = jnp.stack(gather_ring(mine, "y"))
    pieces = jnp.concatenate([pieces, shift(pieces, "c", 1)], 2)

    def product(d):
        rows = lax.dynamic_index_in_dim(
            pieces, lax.rem(x + d - y + ny, ny), 0, keepdims=False
        )
        return jnp.dot(rows, vir_rows, preferred_element_type=jnp.float32).astype(jnp.bfloat16)

    pencil = scatter_sum(product, "x").reshape(each, naux, vir_width)
    mixed = jnp.einsum(
        "qp,kpv->qkv", metric_factor, pencil, preferred_element_type=jnp.float32
    )
    return mixed.astype(jnp.bfloat16)


def solution(mesh):
    aux, ao = mesh.devices.shape
    grid = Mesh(mesh.devices.reshape(4, aux // 4, ao // 2, 2), ("x", "z", "y", "c"))
    every = P()
    return jax.shard_map(
        shards,
        mesh=grid,
        in_specs=(P(("x", "z"), ("y", "c")), every, P(("x", "z"), ("y", "c"))) + (every,) * 5,
        out_specs=P(None, ("x", "z"), ("y", "c")),
        check_vma=False,
    )
```

```python
import jax
import jax.numpy as jnp
from jax import lax
from jax.experimental import pallas as pl
from jax.experimental.pallas import tpu as pltpu
from jax.sharding import Mesh, PartitionSpec as P

GROUP_ROWS = 6


def partial_kernel(
    rows, cols, counts, place, own, other, occ, order, out, total, coef, *, slots, width, blocks_x
):
    y, core = place[0], place[1]
    occ_width = occ.shape[0]
    half_blocks = blocks_x // 2
    pick = lax.broadcasted_iota(jnp.int32, (occ_width, occ_width), 1) == order[...]
    pick = jnp.where(pick, 1.0, 0.0).astype(jnp.bfloat16)
    for row in range(coef.shape[0]):
        chosen = jnp.dot(
            pick, occ[:, row * width : (row + 1) * width], preferred_element_type=jnp.float32
        )
        coef[row] = chosen.astype(jnp.bfloat16)
    total[...] = jnp.zeros_like(total)

    for which, blocks in ((core, own), (1 - core, other)):
        group = 2 * y + which

        @pl.loop(0, counts[group])
        def _(slot):
            col = cols[group * slots + slot]
            inside = lax.rem(col, blocks_x)

            @pl.when(inside // half_blocks == core)
            def _():
                row = rows[group * slots + slot] - 2 * y * GROUP_ROWS
                local = (col // blocks_x) * half_blocks + lax.rem(inside, half_blocks)
                total[local] += jnp.dot(
                    coef[row], blocks[slot], preferred_element_type=jnp.float32
                )

    ny, nx, rows_y, _ = out.shape
    for block in range(total.shape[0]):
        at = block // half_blocks, block % half_blocks * width
        for part in range(ny):
            out[part, at[0], :, at[1] : at[1] + width] = total[
                block, part * rows_y : (part + 1) * rows_y
            ].astype(out.dtype)


def group_partial(own, other, occ_coef, order, rows, cols, counts, place, nx, ny):
    slots, width = own.shape[0], own.shape[1]
    occ_width, ao_width = occ_coef.shape
    half_blocks = ao_width // width // 2
    blocks_x = ao_width // width // nx
    shape = (ny, nx, occ_width // ny, blocks_x // 2 * width)
    kernel = lambda *refs: partial_kernel(*refs, slots=slots, width=width, blocks_x=blocks_x)
    whole = lambda *shape: pl.BlockSpec(shape, lambda i, *_: (0,) * len(shape))
    return pl.pallas_call(
        kernel,
        grid_spec=pltpu.PrefetchScalarGridSpec(
            num_scalar_prefetch=4,
            grid=(1,),
            in_specs=[
                whole(slots, width, width),
                whole(slots, width, width),
                pl.BlockSpec(
                    (occ_width, 2 * GROUP_ROWS * width), lambda i, r, c, n, place: (0, place[0])
                ),
                whole(occ_width, 1),
            ],
            out_specs=whole(*shape),
            scratch_shapes=[
                pltpu.VMEM((half_blocks, occ_width, width), jnp.float32),
                pltpu.VMEM((2 * GROUP_ROWS, occ_width, width), jnp.bfloat16),
            ],
        ),
        out_shape=jax.ShapeDtypeStruct(shape, jnp.bfloat16),
        compiler_params=pltpu.CompilerParams(vmem_limit_bytes=60 << 20),
        name="group_partial",
    )(rows, cols, counts, place, own, other, occ_coef, order)


def shift(value, axis, step):
    n = lax.axis_size(axis)
    return lax.ppermute(value, axis, [(i, (i + step) % n) for i in range(n)])


def swap(value, axis):
    return lax.all_to_all(value, axis, 0, 0, tiled=True)


def scatter_sum(terms, axis):
    return jnp.sum(swap(terms, axis).astype(jnp.float32), 0).astype(jnp.bfloat16)


def gather(mine, axis):
    n = lax.axis_size(axis)
    return swap(jnp.broadcast_to(mine[None], (n,) + mine.shape), axis)


def shards(
    pair_integrals,
    occ_coef,
    vir_coef,
    metric_factor,
    block_rows,
    block_cols,
    block_count,
    occ_order,
):
    x, y, core = lax.axis_index("x"), lax.axis_index("y"), lax.axis_index("c")
    nx, nz, ny = lax.axis_size("x"), lax.axis_size("z"), lax.axis_size("y")
    width = pair_integrals.shape[2]
    occ_width, ao_width = occ_coef.shape
    vir_width = vir_coef.shape[1]
    naux = nx * nz
    each = occ_width // naux
    blocks_x = ao_width // width // nx
    half_blocks = blocks_x // 2

    vir_rows = lax.all_gather(vir_coef, "z", axis=0, tiled=True)

    own = pair_integrals[0]
    other = shift(own, "c", 1)
    order = occ_order.reshape(nx, nz, each).transpose(0, 2, 1).reshape(occ_width, 1)
    place = jnp.stack([y, core]).astype(jnp.int32)
    part = group_partial(
        own, other, occ_coef, order, block_rows, block_cols, block_count, place, nx, ny
    )
    share = scatter_sum(part, "y")
    share = swap(share, "x")
    send = share.reshape(nx, each, nz, half_blocks, width).transpose(2, 0, 1, 3, 4)
    got = swap(send.reshape(nz, nx * each * half_blocks, width), "z")
    got, vir_rows = lax.optimization_barrier((got, vir_rows))
    mine = got.reshape(nz, nx, each, half_blocks, width).transpose(2, 1, 0, 3, 4)
    mine = mine.reshape(each * naux, half_blocks * width)
    held = gather(mine, "y")
    traded = shift(held, "c", 1)
    deep = vir_rows.shape[0] // 2
    terms = jnp.einsum(
        "xmk,kv->xmv",
        held,
        lax.dynamic_slice_in_dim(vir_rows, core * deep, deep, 0),
        preferred_element_type=jnp.float32,
    ) + jnp.einsum(
        "xmk,kv->xmv",
        traded,
        lax.dynamic_slice_in_dim(vir_rows, (1 - core) * deep, deep, 0),
        preferred_element_type=jnp.float32,
    )
    pencil = scatter_sum(terms.astype(jnp.bfloat16), "x").reshape(each, naux, vir_width)
    mixed = jnp.einsum(
        "qp,kpv->qkv", metric_factor, pencil, preferred_element_type=jnp.float32
    )
    return mixed.astype(jnp.bfloat16)


def solution(mesh):
    aux, ao = mesh.devices.shape
    grid = Mesh(mesh.devices.reshape(4, aux // 4, ao // 2, 2), ("x", "z", "y", "c"))
    every = P()
    return jax.shard_map(
        shards,
        mesh=grid,
        in_specs=(P(("x", "z"), ("y", "c")), every, P(("x", "z"), ("y", "c"))) + (every,) * 5,
        out_specs=P(None, ("x", "z"), ("y", "c")),
        check_vma=False,
    )
```

```python
import jax
import jax.numpy as jnp
from jax import lax
from jax.experimental import pallas as pl
from jax.experimental.pallas import tpu as pltpu
from jax.sharding import Mesh, PartitionSpec as P

GROUP_ROWS = 6


def partial_kernel(rows, cols, counts, place, own, other, occ, order, out, total, coef):
    nx, ny, rows_y, half_width = out.shape
    slots, width = own.shape[:2]
    occ_width = occ.shape[0]
    half_blocks = half_width // width
    blocks_x = 2 * half_blocks
    y, core = place[0], place[1]
    pick = lax.broadcasted_iota(jnp.int32, (occ_width, occ_width), 1) == order[...]
    pick = jnp.where(pick, 1.0, 0.0).astype(jnp.bfloat16)
    for row in range(coef.shape[0]):
        chosen = jnp.dot(
            pick, occ[:, row * width : (row + 1) * width], preferred_element_type=jnp.float32
        )
        coef[row] = chosen.astype(coef.dtype)
    total[...] = jnp.zeros_like(total)

    for which, blocks in ((core, own), (1 - core, other)):
        group = 2 * y + which

        @pl.loop(0, counts[group])
        def _(slot):
            col = cols[group * slots + slot]
            inside = lax.rem(col, blocks_x)

            @pl.when(inside // half_blocks == core)
            def _():
                row = rows[group * slots + slot] - 2 * y * GROUP_ROWS
                local = (col // blocks_x) * half_blocks + lax.rem(inside, half_blocks)
                total[local] += jnp.dot(
                    coef[row], blocks[slot], preferred_element_type=jnp.float32
                )

    for block in range(total.shape[0]):
        at = block // half_blocks, block % half_blocks * width
        for part in range(ny):
            out[at[0], part, :, at[1] : at[1] + width] = total[
                block, part * rows_y : (part + 1) * rows_y
            ].astype(out.dtype)


def whole(*shape):
    return pl.BlockSpec(shape, lambda *_: (0,) * len(shape))


def group_partial(own, other, occ_coef, order, rows, cols, counts, place, nx, ny):
    slots, width = own.shape[0], own.shape[1]
    occ_width, ao_width = occ_coef.shape
    half_blocks = ao_width // width // 2
    chip_rows = 2 * GROUP_ROWS
    shape = (nx, ny, occ_width // ny, half_blocks // nx * width)
    return pl.pallas_call(
        partial_kernel,
        grid_spec=pltpu.PrefetchScalarGridSpec(
            num_scalar_prefetch=4,
            grid=(1,),
            in_specs=[
                whole(slots, width, width),
                whole(slots, width, width),
                pl.BlockSpec((occ_width, chip_rows * width), lambda i, r, c, n, place: (0, place[0])),
                whole(occ_width, 1),
            ],
            out_specs=whole(*shape),
            scratch_shapes=[
                pltpu.VMEM((half_blocks, occ_width, width), jnp.float32),
                pltpu.VMEM((chip_rows, occ_width, width), jnp.bfloat16),
            ],
        ),
        out_shape=jax.ShapeDtypeStruct(shape, jnp.bfloat16),
        compiler_params=pltpu.CompilerParams(vmem_limit_bytes=60 << 20),
        name="group_partial",
    )(rows, cols, counts, place, own, other, occ_coef, order)


def halves_kernel(place, rows, out, done):
    half = rows.shape[0] // 2
    copies = []
    for part, which in enumerate((place[1], 1 - place[1])):
        source = rows.at[pl.ds(pl.multiple_of(which * half, half), half)]
        copies.append(
            pltpu.make_async_copy(source, out.at[pl.ds(part * half, half)], done.at[part])
        )
    for copy in copies:
        copy.start()
    for copy in copies:
        copy.wait()


def halves(rows, place):
    return pl.pallas_call(
        halves_kernel,
        grid_spec=pltpu.PrefetchScalarGridSpec(
            num_scalar_prefetch=1,
            grid=(1,),
            in_specs=[pl.BlockSpec(memory_space=pl.ANY)],
            out_specs=whole(*rows.shape),
            scratch_shapes=[pltpu.SemaphoreType.DMA((2,))],
        ),
        out_shape=jax.ShapeDtypeStruct(rows.shape, rows.dtype),
        compiler_params=pltpu.CompilerParams(vmem_limit_bytes=16 << 20),
        cost_estimate=pl.CostEstimate(flops=0, bytes_accessed=4 << 20, transcendentals=0),
        name="vir_halves",
    )(place, rows)


def product_kernel(held, traded, coef, out):
    half, cut = held.shape[2], coef.shape[1]
    total = jnp.dot(held[0], coef[:half], preferred_element_type=jnp.float32)
    total += jnp.dot(traded[0], coef[half:], preferred_element_type=jnp.float32)
    out[0, :, :cut] = total.astype(out.dtype)
    if cut < out.shape[2]:
        out[0, :, cut:] = jnp.zeros((total.shape[0], out.shape[2] - cut), out.dtype)


def product(held, traded, coef, lanes):
    n, rows, half = held.shape
    width = pl.cdiv(coef.shape[1], lanes) * lanes
    block = lambda cols: pl.BlockSpec((1, rows, cols), lambda i: (i, 0, 0))
    return pl.pallas_call(
        product_kernel,
        grid=(n,),
        in_specs=[block(half), block(half), whole(*coef.shape)],
        out_specs=block(width),
        out_shape=jax.ShapeDtypeStruct((n, rows, width), jnp.bfloat16),
        compiler_params=pltpu.CompilerParams(vmem_limit_bytes=24 << 20),
        cost_estimate=pl.CostEstimate(
            flops=4 * n * rows * half * width, bytes_accessed=8 << 20, transcendentals=0
        ),
        name="product",
    )(held, traded, coef)


def shift(value, axis, step):
    n = lax.axis_size(axis)
    return lax.ppermute(value, axis, [(i, (i + step) % n) for i in range(n)])


def swap(value, axis):
    return lax.all_to_all(value, axis, 0, 0, tiled=True)


def gather(mine, axis):
    n = lax.axis_size(axis)
    return swap(jnp.broadcast_to(mine[None], (n,) + mine.shape), axis)


def shards(
    pair_integrals,
    occ_coef,
    vir_coef,
    metric_factor,
    block_rows,
    block_cols,
    block_count,
    occ_order,
):
    y, core = lax.axis_index("y"), lax.axis_index("c")
    nx, nz, ny = lax.axis_size("x"), lax.axis_size("z"), lax.axis_size("y")
    width = pair_integrals.shape[2]
    occ_width, ao_width = occ_coef.shape
    vir_width = vir_coef.shape[1]
    naux = nx * nz
    each = occ_width // naux
    place = jnp.stack([y, core]).astype(jnp.int32)

    own = pair_integrals[0]
    other = shift(own, "c", 1)
    order = occ_order.reshape(nx, nz, each).transpose(0, 2, 1).reshape(occ_width, 1)
    part = group_partial(
        own, other, occ_coef, order, block_rows, block_cols, block_count, place, nx, ny
    )
    vir_rows = lax.all_gather(vir_coef, "z", axis=0, tiled=True)
    share = swap(part.reshape((nx * ny,) + part.shape[2:]), ("x", "y")).reshape(part.shape)
    share = jnp.sum(share.astype(jnp.float32), 1).astype(jnp.bfloat16)
    held = gather(share.reshape(-1, share.shape[-1]), "y")
    held, vir_rows = lax.optimization_barrier((held, vir_rows))
    traded = shift(held, "c", 1)
    terms = swap(product(held, traded, halves(vir_rows, place), width), "x")
    pencil = jnp.sum(terms.astype(jnp.float32), 0).astype(jnp.bfloat16)
    pencil = pencil.reshape(nx, each, nz, -1, width).transpose(2, 0, 1, 3, 4)
    pencil = swap(pencil.reshape(nz, -1, width), "z")
    pencil = pencil.reshape(nz, nx, each, -1, width).transpose(2, 1, 0, 3, 4)
    pencil = pencil.reshape(each, naux, -1)[:, :, :vir_width]
    mixed = jnp.einsum("qp,kpv->qkv", metric_factor, pencil, preferred_element_type=jnp.float32)
    return mixed.astype(jnp.bfloat16)


def solution(mesh):
    aux, ao = mesh.devices.shape
    grid = Mesh(mesh.devices.reshape(4, aux // 4, ao // 2, 2), ("x", "z", "y", "c"))
    every = P()
    return jax.shard_map(
        shards,
        mesh=grid,
        in_specs=(P(("x", "z"), ("y", "c")), every, P(("x", "z"), ("y", "c"))) + (every,) * 5,
        out_specs=P(None, ("x", "z"), ("y", "c")),
        check_vma=False,
    )
```

```python
import jax
import jax.numpy as jnp
from jax import lax
from jax.experimental import pallas as pl
from jax.experimental.pallas import tpu as pltpu
from jax.sharding import Mesh, PartitionSpec as P

GROUP_ROWS = 6


def partial_kernel(rows, cols, counts, place, own, other, occ, order, out, total, coef):
    nx, ny, rows_y, half_width = out.shape
    slots, width = own.shape[:2]
    occ_width = occ.shape[0]
    half_blocks = half_width // width
    blocks_x = 2 * half_blocks
    y, core = place[0], place[1]
    pick = lax.broadcasted_iota(jnp.int32, (occ_width, occ_width), 1) == order[...]
    pick = jnp.where(pick, 1.0, 0.0).astype(jnp.bfloat16)
    for row in range(coef.shape[0]):
        chosen = jnp.dot(
            pick, occ[:, row * width : (row + 1) * width], preferred_element_type=jnp.float32
        )
        coef[row] = chosen.astype(coef.dtype)
    total[...] = jnp.zeros_like(total)

    for which, blocks in ((core, own), (1 - core, other)):
        group = 2 * y + which

        @pl.loop(0, counts[group])
        def _(slot):
            col = cols[group * slots + slot]
            inside = lax.rem(col, blocks_x)

            @pl.when(inside // half_blocks == core)
            def _():
                row = rows[group * slots + slot] - 2 * y * GROUP_ROWS
                local = (col // blocks_x) * half_blocks + lax.rem(inside, half_blocks)
                total[local] += jnp.dot(
                    coef[row], blocks[slot], preferred_element_type=jnp.float32
                )

    for block in range(total.shape[0]):
        at = block // half_blocks, block % half_blocks * width
        for part in range(ny):
            out[at[0], part, :, at[1] : at[1] + width] = total[
                block, part * rows_y : (part + 1) * rows_y
            ].astype(out.dtype)


def whole(*shape):
    return pl.BlockSpec(shape, lambda *_: (0,) * len(shape))


def group_partial(own, other, occ_coef, order, rows, cols, counts, place, nx, ny):
    slots, width = own.shape[0], own.shape[1]
    occ_width, ao_width = occ_coef.shape
    half_blocks = ao_width // width // 2
    chip_rows = 2 * GROUP_ROWS
    shape = (nx, ny, occ_width // ny, half_blocks // nx * width)
    return pl.pallas_call(
        partial_kernel,
        grid_spec=pltpu.PrefetchScalarGridSpec(
            num_scalar_prefetch=4,
            grid=(1,),
            in_specs=[
                whole(slots, width, width),
                whole(slots, width, width),
                pl.BlockSpec((occ_width, chip_rows * width), lambda i, r, c, n, place: (0, place[0])),
                whole(occ_width, 1),
            ],
            out_specs=whole(*shape),
            scratch_shapes=[
                pltpu.VMEM((half_blocks, occ_width, width), jnp.float32),
                pltpu.VMEM((chip_rows, occ_width, width), jnp.bfloat16),
            ],
        ),
        out_shape=jax.ShapeDtypeStruct(shape, jnp.bfloat16),
        compiler_params=pltpu.CompilerParams(vmem_limit_bytes=60 << 20),
        name="group_partial",
    )(rows, cols, counts, place, own, other, occ_coef, order)


def halves_kernel(place, rows, out, done):
    half = rows.shape[0] // 2
    copies = []
    for part, which in enumerate((place[1], 1 - place[1])):
        source = rows.at[pl.ds(pl.multiple_of(which * half, half), half)]
        copies.append(
            pltpu.make_async_copy(source, out.at[pl.ds(part * half, half)], done.at[part])
        )
    for copy in copies:
        copy.start()
    for copy in copies:
        copy.wait()


def halves(rows, place):
    return pl.pallas_call(
        halves_kernel,
        grid_spec=pltpu.PrefetchScalarGridSpec(
            num_scalar_prefetch=1,
            grid=(1,),
            in_specs=[pl.BlockSpec(memory_space=pl.ANY)],
            out_specs=whole(*rows.shape),
            scratch_shapes=[pltpu.SemaphoreType.DMA((2,))],
        ),
        out_shape=jax.ShapeDtypeStruct(rows.shape, rows.dtype),
        compiler_params=pltpu.CompilerParams(vmem_limit_bytes=16 << 20),
        cost_estimate=pl.CostEstimate(flops=0, bytes_accessed=4 << 20, transcendentals=0),
        name="vir_halves",
    )(place, rows)


def product_kernel(held, traded, coef, out):
    half, cut = held.shape[2], coef.shape[1]
    total = jnp.dot(held[0], coef[:half], preferred_element_type=jnp.float32)
    total += jnp.dot(traded[0], coef[half:], preferred_element_type=jnp.float32)
    out[0, :, :cut] = total.astype(out.dtype)
    if cut < out.shape[2]:
        out[0, :, cut:] = jnp.zeros((total.shape[0], out.shape[2] - cut), out.dtype)


def product(held, traded, coef, lanes):
    n, rows, half = held.shape
    width = pl.cdiv(coef.shape[1], lanes) * lanes
    block = lambda cols: pl.BlockSpec((1, rows, cols), lambda i: (i, 0, 0))
    return pl.pallas_call(
        product_kernel,
        grid=(n,),
        in_specs=[block(half), block(half), whole(*coef.shape)],
        out_specs=block(width),
        out_shape=jax.ShapeDtypeStruct((n, rows, width), jnp.bfloat16),
        compiler_params=pltpu.CompilerParams(vmem_limit_bytes=24 << 20),
        cost_estimate=pl.CostEstimate(
            flops=4 * n * rows * half * width, bytes_accessed=8 << 20, transcendentals=0
        ),
        name="product",
    )(held, traded, coef)


def shift(value, axis, step):
    n = lax.axis_size(axis)
    return lax.ppermute(value, axis, [(i, (i + step) % n) for i in range(n)])


def swap(value, axis):
    return lax.all_to_all(value, axis, 0, 0, tiled=True)


def gather(mine, axis):
    n = lax.axis_size(axis)
    return swap(jnp.broadcast_to(mine[None], (n,) + mine.shape), axis)


def shards(
    pair_integrals,
    occ_coef,
    vir_coef,
    metric_factor,
    block_rows,
    block_cols,
    block_count,
    occ_order,
):
    y, core = lax.axis_index("y"), lax.axis_index("c")
    nx, nz, ny = lax.axis_size("x"), lax.axis_size("z"), lax.axis_size("y")
    width = pair_integrals.shape[2]
    occ_width, ao_width = occ_coef.shape
    vir_width = vir_coef.shape[1]
    naux = nx * nz
    each = occ_width // naux
    place = jnp.stack([y, core]).astype(jnp.int32)

    own = pair_integrals[0]
    other = shift(own, "c", 1)
    order = occ_order.reshape(nx, nz, each).transpose(0, 2, 1).reshape(occ_width, 1)
    part = group_partial(
        own, other, occ_coef, order, block_rows, block_cols, block_count, place, nx, ny
    )
    part, vir_coef = lax.optimization_barrier((part, vir_coef))
    vir_rows = lax.all_gather(vir_coef, "z", axis=0, tiled=True)
    def exchange(value):
        terms = swap(value, ("x", "y")).reshape(part.shape)
        return jnp.sum(terms.astype(jnp.float32), 1).astype(jnp.bfloat16)

    share = lax.cond(
        jnp.max(block_count) > 0,
        exchange,
        lambda value: jnp.zeros((nx,) + part.shape[2:], jnp.bfloat16),
        part.reshape((nx * ny,) + part.shape[2:]),
    )
    held = gather(share.reshape(-1, share.shape[-1]), "y")
    traded = shift(held, "c", 1)
    terms = swap(product(held, traded, halves(vir_rows, place), width), "x")
    pencil = jnp.sum(terms.astype(jnp.float32), 0).astype(jnp.bfloat16)
    pencil = pencil.reshape(nx, each, nz, -1, width).transpose(2, 0, 1, 3, 4)
    pencil = swap(pencil.reshape(nz, -1, width), "z")
    pencil = pencil.reshape(nz, nx, each, -1, width).transpose(2, 1, 0, 3, 4)
    pencil = pencil.reshape(each, naux, -1)[:, :, :vir_width]
    mixed = jnp.einsum("qp,kpv->qkv", metric_factor, pencil, preferred_element_type=jnp.float32)
    return mixed.astype(jnp.bfloat16)


def solution(mesh):
    aux, ao = mesh.devices.shape
    grid = Mesh(mesh.devices.reshape(4, aux // 4, ao // 2, 2), ("x", "z", "y", "c"))
    every = P()
    return jax.shard_map(
        shards,
        mesh=grid,
        in_specs=(P(("x", "z"), ("y", "c")), every, P(("x", "z"), ("y", "c"))) + (every,) * 5,
        out_specs=P(None, ("x", "z"), ("y", "c")),
        check_vma=False,
    )
```

```python
import jax
import jax.numpy as jnp
from jax import lax
from jax.experimental import pallas as pl
from jax.experimental.pallas import tpu as pltpu
from jax.sharding import Mesh, PartitionSpec as P

GROUP_ROWS = 6


def partial_kernel(rows, cols, counts, place, own, other, occ, order, out, total, coef):
    nx, ny, rows_y, half_width = out.shape
    slots, width = own.shape[:2]
    occ_width = occ.shape[0]
    half_blocks = half_width // width
    blocks_x = 2 * half_blocks
    y, core = place[0], place[1]
    pick = lax.broadcasted_iota(jnp.int32, (occ_width, occ_width), 1) == order[...]
    pick = jnp.where(pick, 1.0, 0.0).astype(jnp.bfloat16)
    for row in range(0, coef.shape[0], 2):
        chosen = jnp.dot(
            pick, occ[:, row * width : (row + 2) * width], preferred_element_type=jnp.float32
        ).astype(coef.dtype)
        coef[row] = chosen[:, :width]
        coef[row + 1] = chosen[:, width:]
    total[...] = jnp.zeros_like(total)

    for which, blocks in ((core, own), (1 - core, other)):
        group = 2 * y + which

        @pl.loop(0, counts[group])
        def _(slot):
            col = cols[group * slots + slot]
            inside = lax.rem(col, blocks_x)

            @pl.when(inside // half_blocks == core)
            def _():
                row = rows[group * slots + slot] - 2 * y * GROUP_ROWS
                local = (col // blocks_x) * half_blocks + lax.rem(inside, half_blocks)
                total[local] += jnp.dot(
                    coef[row], blocks[slot], preferred_element_type=jnp.float32
                )

    for block in range(total.shape[0]):
        at = block // half_blocks, block % half_blocks * width
        for part in range(ny):
            out[at[0], part, :, at[1] : at[1] + width] = total[
                block, part * rows_y : (part + 1) * rows_y
            ].astype(out.dtype)


def whole(*shape):
    return pl.BlockSpec(shape, lambda *_: (0,) * len(shape))


def group_partial(own, other, occ_coef, order, rows, cols, counts, place, nx, ny):
    slots, width = own.shape[0], own.shape[1]
    occ_width, ao_width = occ_coef.shape
    half_blocks = ao_width // width // 2
    chip_rows = 2 * GROUP_ROWS
    shape = (nx, ny, occ_width // ny, half_blocks // nx * width)
    return pl.pallas_call(
        partial_kernel,
        grid_spec=pltpu.PrefetchScalarGridSpec(
            num_scalar_prefetch=4,
            grid=(1,),
            in_specs=[
                whole(slots, width, width),
                whole(slots, width, width),
                pl.BlockSpec((occ_width, chip_rows * width), lambda i, r, c, n, place: (0, place[0])),
                whole(occ_width, 1),
            ],
            out_specs=whole(*shape),
            scratch_shapes=[
                pltpu.VMEM((half_blocks, occ_width, width), jnp.float32),
                pltpu.VMEM((chip_rows, occ_width, width), jnp.bfloat16),
            ],
        ),
        out_shape=jax.ShapeDtypeStruct(shape, jnp.bfloat16),
        compiler_params=pltpu.CompilerParams(vmem_limit_bytes=60 << 20),
        name="group_partial",
    )(rows, cols, counts, place, own, other, occ_coef, order)


def halves_kernel(place, rows, out, done):
    half = rows.shape[0] // 2
    copies = []
    for part, which in enumerate((place[1], 1 - place[1])):
        source = rows.at[pl.ds(pl.multiple_of(which * half, half), half)]
        copies.append(
            pltpu.make_async_copy(source, out.at[pl.ds(part * half, half)], done.at[part])
        )
    for copy in copies:
        copy.start()
    for copy in copies:
        copy.wait()


def halves(rows, place):
    return pl.pallas_call(
        halves_kernel,
        grid_spec=pltpu.PrefetchScalarGridSpec(
            num_scalar_prefetch=1,
            grid=(1,),
            in_specs=[pl.BlockSpec(memory_space=pl.ANY)],
            out_specs=whole(*rows.shape),
            scratch_shapes=[pltpu.SemaphoreType.DMA((2,))],
        ),
        out_shape=jax.ShapeDtypeStruct(rows.shape, rows.dtype),
        compiler_params=pltpu.CompilerParams(vmem_limit_bytes=16 << 20),
        cost_estimate=pl.CostEstimate(flops=0, bytes_accessed=4 << 20, transcendentals=0),
        name="vir_halves",
    )(place, rows)


def product_kernel(held, traded, coef, out):
    (many, rows, half), cut = held.shape, coef.shape[1]
    flat = lambda ref: ref[...].reshape(many * rows, half)
    total = jnp.dot(flat(held), coef[:half], preferred_element_type=jnp.float32)
    total += jnp.dot(flat(traded), coef[half:], preferred_element_type=jnp.float32)
    out[:, :, :cut] = total.astype(out.dtype).reshape(many, rows, cut)
    if cut < out.shape[2]:
        out[:, :, cut:] = jnp.zeros((many, rows, out.shape[2] - cut), out.dtype)


def product(held, traded, coef, lanes):
    n, rows, half = held.shape
    width = pl.cdiv(coef.shape[1], lanes) * lanes
    block = lambda cols: pl.BlockSpec((2, rows, cols), lambda i: (i, 0, 0))
    return pl.pallas_call(
        product_kernel,
        grid=(n // 2,),
        in_specs=[block(half), block(half), whole(*coef.shape)],
        out_specs=block(width),
        out_shape=jax.ShapeDtypeStruct((n, rows, width), jnp.bfloat16),
        compiler_params=pltpu.CompilerParams(vmem_limit_bytes=24 << 20),
        cost_estimate=pl.CostEstimate(
            flops=4 * n * rows * half * width, bytes_accessed=8 << 20, transcendentals=0
        ),
        name="product",
    )(held, traded, coef)


def shift(value, axis, step):
    n = lax.axis_size(axis)
    return lax.ppermute(value, axis, [(i, (i + step) % n) for i in range(n)])


def swap(value, axis):
    return lax.all_to_all(value, axis, 0, 0, tiled=True)


def gather(mine, axis):
    n = lax.axis_size(axis)
    return swap(jnp.broadcast_to(mine[None], (n,) + mine.shape), axis)


def shards(
    pair_integrals,
    occ_coef,
    vir_coef,
    metric_factor,
    block_rows,
    block_cols,
    block_count,
    occ_order,
):
    y, core = lax.axis_index("y"), lax.axis_index("c")
    nx, nz, ny = lax.axis_size("x"), lax.axis_size("z"), lax.axis_size("y")
    width = pair_integrals.shape[2]
    occ_width, ao_width = occ_coef.shape
    vir_width = vir_coef.shape[1]
    naux = nx * nz
    each = occ_width // naux
    place = jnp.stack([y, core]).astype(jnp.int32)

    own = pair_integrals[0]
    other = shift(own, "c", 1)
    order = occ_order.reshape(nx, nz, each).transpose(0, 2, 1).reshape(occ_width, 1)
    part = group_partial(
        own, other, occ_coef, order, block_rows, block_cols, block_count, place, nx, ny
    )
    part, vir_coef = lax.optimization_barrier((part, vir_coef))
    vir_rows = lax.all_gather(vir_coef, "z", axis=0, tiled=True)
    def exchange(value):
        terms = swap(value, ("x", "y")).reshape(part.shape)
        return jnp.sum(terms.astype(jnp.float32), 1).astype(jnp.bfloat16)

    share = lax.cond(
        jnp.max(block_count) > 0,
        exchange,
        lambda value: jnp.zeros((nx,) + part.shape[2:], jnp.bfloat16),
        part.reshape((nx * ny,) + part.shape[2:]),
    )
    held = gather(share.reshape(-1, share.shape[-1]), "y")
    traded = shift(held, "c", 1)
    terms = swap(product(held, traded, halves(vir_rows, place), width), "x")
    pencil = jnp.sum(terms.astype(jnp.float32), 0).astype(jnp.bfloat16)
    pencil = pencil.reshape(nx, each, nz, -1, width).transpose(2, 0, 1, 3, 4)
    pencil = swap(pencil.reshape(nz, -1, width), "z")
    pencil = pencil.reshape(nz, nx, each, -1, width).transpose(2, 1, 0, 3, 4)
    pencil = pencil.reshape(each, naux, -1)[:, :, :vir_width]
    mixed = jnp.einsum("qp,kpv->qkv", metric_factor, pencil, preferred_element_type=jnp.float32)
    return mixed.astype(jnp.bfloat16)


def solution(mesh):
    aux, ao = mesh.devices.shape
    grid = Mesh(mesh.devices.reshape(4, aux // 4, ao // 2, 2), ("x", "z", "y", "c"))
    every = P()
    return jax.shard_map(
        shards,
        mesh=grid,
        in_specs=(P(("x", "z"), ("y", "c")), every, P(("x", "z"), ("y", "c"))) + (every,) * 5,
        out_specs=P(None, ("x", "z"), ("y", "c")),
        check_vma=False,
    )
```
